32 devices in a mesh: rep: 2 (over core), tx: 4 (over y, x), ty: 4 (over z).
Axes of the slice: x: 2, y: 2, z: 4, core: 2. Of those that a mesh axis runs over, the one named last changes fastest.
Arguments:
- queries: bfloat16 [2, 32, 32, 4, 384], P('rep', 'tx', 'ty'), may hold values from -8 to 8
- keys: bfloat16 [2, 32, 32, 4, 384], P('rep', 'tx', 'ty'), may hold values from -8 to 8
- values: bfloat16 [2, 32, 32, 4, 384], P('rep', 'tx', 'ty'), may hold values from -6 to 6
- grad_out: bfloat16 [2, 32, 32, 4, 768], P('rep', 'tx', 'ty'), may hold values from -6 to 6
- w_out: bfloat16 [384, 768], replicated, may hold values from -0.3125 to 0.3125
- fluid_count: int32 [4, 4], P('tx', 'ty'), may hold values from 64 to 256, as said below
Outputs:
- grad_q: bfloat16 [2, 32, 32, 4, 384], P('rep', 'tx', 'ty')
- grad_k: bfloat16 [2, 32, 32, 4, 384], P('rep', 'tx', 'ty')
- grad_v: bfloat16 [2, 32, 32, 4, 384], P('rep', 'tx', 'ty')
- grad_w: float32 [384, 768], replicated
The draws below stay inside these ranges and needn't reach their ends.
Inputs may be any that keep to these rules, and one draw needn't show every extreme that they name: `fluid_count`: some window has 256 fluid cells and another 8 * 8 in every draw.
All inputs are finite; a program needn't handle non-finite values.
Results may differ from the reference program's by a relative error of at most 0.011.
Values may be sent and summed in bfloat16 or wider, within the bound.
A program may use at most 64 MiB of HBM per device.

```python
import math
import jax
import jax.numpy as jnp
from jax import lax

D = 768
HEADS = 12
HEAD_DIM = 32
WIN = 8
DH = 384
WINDOW = 256
SHIFT = 4
BATCH = 2
NWX = 4
NWY = 4
NX = 32
NY = 32
NZ = 4
TOKENS = 8192


def draw_queries(key, part):
    base = jax.random.normal(jax.random.fold_in(key, 1), (BATCH, NX, NY, NZ, HEADS * HEAD_DIM), jnp.float32)
    base = jnp.clip(base, -6.0, 6.0)
    return base.astype(jnp.bfloat16)


def draw_keys(key, part):
    base = jax.random.normal(jax.random.fold_in(key, 2), (BATCH, NX, NY, NZ, HEADS * HEAD_DIM), jnp.float32)
    base = jnp.clip(base, -6.0, 6.0)
    return base.astype(jnp.bfloat16)


def draw_fluid_count(key, part):
    total_windows = NWX * NWY
    counts = jax.random.randint(jax.random.fold_in(key, 3), (total_windows,), WIN * WIN, WINDOW + 1)
    full_spot = jax.random.randint(jax.random.fold_in(key, 5), (), 0, total_windows)
    offset = jax.random.randint(jax.random.fold_in(key, 6), (), 0, total_windows - 1)
    other_spot = (full_spot + 1 + offset) % total_windows
    counts = counts.at[full_spot].set(WINDOW).at[other_spot].set(WIN * WIN)
    return counts.reshape(NWX, NWY).astype(jnp.int32)


def block_scale(stream_key, shape, shards, least, largest):
    factor_of, own = 1.0, jax.random.fold_in(stream_key, 6)
    for position, parts in shards:
        steps = jnp.exp(jax.random.uniform(jax.random.fold_in(own, position), (parts,), jnp.float32, least / len(shards), largest / len(shards)))
        factor_of = factor_of * jnp.repeat(steps, shape[position] // parts).reshape([-1 if axis == position else 1 for axis in range(len(shape))])
    return factor_of


def noise(key, dims, spread, bound, cuts=(), kind=jnp.bfloat16):
    factor_of = block_scale(key, dims, cuts, -0.22, 0.18) if cuts else 1.0
    values = jax.random.normal(key, dims, jnp.float32) * spread * factor_of
    return jnp.minimum(jnp.maximum(values, -bound), bound).astype(kind)


def setup_inputs(seed: int = 0) -> dict:
    seeds = jax.random.split(jax.random.key(seed), 7)
    queries = draw_queries(jax.random.fold_in(seeds[6], 71), 0)
    keys = draw_keys(jax.random.fold_in(seeds[6], 71), 0)
    values = noise(seeds[2], (BATCH, NX, NY, NZ, DH), 1.0, 6.0, ((0, 2), (1, 4), (2, 4)))
    grad_out = noise(seeds[3], (BATCH, NX, NY, NZ, D), 1.0, 6.0, ((0, 2), (1, 4), (2, 4)))
    w_out = noise(seeds[4], (DH, D), DH ** -0.5, 0.3125)
    fluid_count = draw_fluid_count(jax.random.fold_in(seeds[6], 71), 0)
    return dict(queries=queries, keys=keys, values=values, grad_out=grad_out, w_out=w_out, fluid_count=fluid_count)


NEG_FILL = -1e+30

def window_grads(q_rows, k_rows, v_rows, d_rows, fluid_total):
    row_count = q_rows.shape[0]
    head_count = q_rows.shape[1] // HEAD_DIM
    score_scale = HEAD_DIM ** (-0.5)
    is_fluid = lax.iota(jnp.int32, row_count) < fluid_total
    query_heads = q_rows.astype(jnp.float32).reshape(row_count, head_count, HEAD_DIM)
    key_heads = k_rows.astype(jnp.float32).reshape(row_count, head_count, HEAD_DIM)
    value_heads = v_rows.astype(jnp.float32).reshape(row_count, head_count, HEAD_DIM)
    grad_heads = d_rows.astype(jnp.float32).reshape(row_count, head_count, HEAD_DIM)
    scores = jnp.einsum('qhd,khd->hqk', query_heads, key_heads) * score_scale
    scores = jnp.where(is_fluid[None, None, :], scores, NEG_FILL)
    row_peak = lax.optimization_barrier(jnp.max(scores, axis=2, keepdims=True))
    exponent = jnp.exp(scores - row_peak)
    soft_weights = exponent / lax.optimization_barrier(jnp.sum(exponent, axis=2, keepdims=True))
    soft_weights = jnp.where(is_fluid[None, :, None], soft_weights, 0.0)
    weights_low = soft_weights.astype(jnp.bfloat16).astype(jnp.float32)
    attn_out = jnp.einsum('hqk,khd->qhd', weights_low, value_heads)
    grad_weights = jnp.einsum('qhd,khd->hqk', grad_heads, value_heads)
    row_delta = lax.optimization_barrier(jnp.sum(soft_weights * grad_weights, axis=2, keepdims=True))
    grad_scores = (soft_weights * (grad_weights - row_delta)).astype(jnp.bfloat16).astype(jnp.float32)
    grad_value = jnp.einsum('hqk,qhd->khd', weights_low, grad_heads)
    grad_query = jnp.einsum('hqk,khd->qhd', grad_scores, key_heads) * score_scale
    grad_key = jnp.einsum('hqk,qhd->khd', grad_scores, query_heads) * score_scale
    width = head_count * HEAD_DIM
    return (attn_out.reshape(row_count, width), grad_query.reshape(row_count, width), grad_key.reshape(row_count, width), grad_value.reshape(row_count, width))

def to_windows(field):
    channels = field.shape[-1]
    blocked = field.reshape(BATCH, NWX, WIN, NWY, WIN, NZ, channels)
    blocked = blocked.transpose(0, 1, 3, 2, 4, 5, 6)
    return blocked.reshape(BATCH * NWX * NWY, WINDOW, channels)

def from_windows(blocks):
    channels = blocks.shape[-1]
    grid = blocks.reshape(BATCH, NWX, NWY, WIN, WIN, NZ, channels).transpose(0, 1, 3, 2, 4, 5, 6)
    return grid.reshape(BATCH, NX, NY, NZ, channels)

def roll_grid(field, amount):
    return jnp.roll(field, (amount, amount), axis=(1, 2))

def reference(queries, keys, values, grad_out, w_out, fluid_count):
    win_q = to_windows(roll_grid(queries, -SHIFT))
    win_k = to_windows(roll_grid(keys, -SHIFT))
    win_v = to_windows(roll_grid(values, -SHIFT))
    win_g = to_windows(roll_grid(grad_out, -SHIFT))
    totals = jnp.broadcast_to(fluid_count[None], (BATCH, NWX, NWY)).reshape(-1).astype(jnp.int32)

    def step_fn(carry, item):
        q_rows, k_rows, v_rows, g_rows, fluid_total = item
        d_rows = jnp.dot(g_rows, w_out.T, preferred_element_type=jnp.float32).astype(jnp.bfloat16)
        attn_out, grad_query, grad_key, grad_value = window_grads(q_rows, k_rows, v_rows, d_rows, fluid_total)
        attn_low = attn_out.astype(jnp.bfloat16)
        term = jnp.dot(attn_low.T, g_rows, preferred_element_type=jnp.float32)
        return (carry + term, (grad_query.astype(jnp.bfloat16), grad_key.astype(jnp.bfloat16), grad_value.astype(jnp.bfloat16)))
    weight_total, outputs = lax.scan(step_fn, jnp.zeros((DH, D), jnp.float32), (win_q, win_k, win_v, win_g, totals))
    grad_q = roll_grid(from_windows(outputs[0]), SHIFT)
    grad_k = roll_grid(from_windows(outputs[1]), SHIFT)
    grad_v = roll_grid(from_windows(outputs[2]), SHIFT)
    grad_w = weight_total * (1.0 / math.sqrt(TOKENS))
    return (grad_q, grad_k, grad_v, grad_w)
```

```python
import functools
import math

import jax
import jax.numpy as jnp
from jax import lax
from jax.experimental import pallas as pl
from jax.experimental.pallas import tpu as pltpu
from jax.sharding import PartitionSpec as P

HEAD_DIM = 32
LANES = 128
PER_GROUP = LANES // HEAD_DIM
NEG_FILL = -1e30
MESH = pl.DeviceIdType.MESH
F32 = jnp.float32
BF16 = jnp.bfloat16


def dot(a, b, dims):
    return lax.dot_general(a, b, (dims, ((), ())), preferred_element_type=F32)


def kernel(plan, fluid, q_in, k_in, v_in, g_in, w_ref, oq, ok, ov, ow, *scratch):
    nx, ny, share, cells = plan
    (qw, kw, vw, gw, probs, dw, gq, gk, gv, in_send, in_recv, own_sem, out_send, out_recv) = scratch[:14]
    rep, tx, ty = lax.axis_index("rep"), lax.axis_index("tx"), lax.axis_index("ty")

    def at(dx, dy):
        return {"tx": lax.rem(tx + dx, nx), "ty": lax.rem(ty + dy, ny)}

    ahead = [at(1, 0), at(0, 1), at(1, 1)]
    behind = [at(nx - 1, 0), at(0, ny - 1), at(nx - 1, ny - 1)]
    if share:
        greet = [{"rep": 1 - rep}, ahead[2], behind[2]]
        greet += [at(d, 0) for d in range(1, nx)] + [at(0, d) for d in range(1, ny)]
    else:
        greet = ahead + behind
    barrier = pltpu.get_barrier_semaphore()
    for peer in greet:
        pl.semaphore_signal(barrier, inc=1, device_id=peer, device_id_type=MESH)

    side, row, width = qw.shape
    hs, hr = side // 2, row // 2
    lo = (slice(0, hs), slice(0, hr))
    low_x = (slice(0, hs), slice(hr, row))
    low_y = (slice(hs, side), slice(0, hr))
    high = (slice(hs, side), slice(hr, row))
    leaving = [(low_x, low_y), (low_y, low_x), (lo, high)]

    fields = [(q_in, qw), (k_in, kw), (v_in, vw), (g_in, gw)]
    owns = []
    for f, (src, dst) in enumerate(fields):
        owns.append(pltpu.make_async_copy(src.at[high], dst.at[lo], own_sem.at[f]))
        owns[-1].start()
    pl.semaphore_wait(barrier, len(greet))
    arriving = []
    for f, (src, dst) in enumerate(fields):
        copies = []
        for n, (from_, to) in enumerate(leaving):
            copies.append(
                pltpu.make_async_remote_copy(
                    src_ref=src.at[from_], dst_ref=dst.at[to],
                    send_sem=in_send.at[f, n], recv_sem=in_recv.at[f, n],
                    device_id=behind[n], device_id_type=MESH,
                )
            )
            copies[-1].start()
        arriving.append(copies)

    def arrive(f):
        owns[f].wait()
        for copy in arriving[f]:
            copy.wait_recv()

    cells_here = side * row
    groups = width // LANES
    count = fluid[0, 0]
    key_ok = lax.broadcasted_iota(jnp.int32, (cells_here, 1), 0) < count
    query_ok = jnp.where(lax.broadcasted_iota(jnp.int32, (1, cells_here), 1) < count, 1.0, 0.0)
    lane_head = lax.broadcasted_iota(jnp.int32, (1, LANES), 1) // HEAD_DIM
    pick = [jnp.where(lane_head == h, 1.0, 0.0).astype(BF16) for h in range(PER_GROUP)]
    scale = HEAD_DIM ** (-0.5)

    def part(ref, g):
        return ref[:, :, g * LANES : (g + 1) * LANES].reshape(cells_here, LANES)

    def attend(g):
        keys, queries = part(kw, g), part(qw, g)
        for h in range(PER_GROUP):
            s = dot(keys, queries * pick[h], ((1,), (1,)))
            s = jnp.where(key_ok, s, NEG_FILL)
            e = jnp.exp2((s - jnp.max(s, axis=0, keepdims=True)) * (scale * math.log2(math.e)))
            inv = query_ok / jnp.sum(e, axis=0, keepdims=True)
            probs[g * PER_GROUP + h] = e * inv

    def mix(g):
        values_t = part(vw, g).T
        outs = []
        for h in range(PER_GROUP):
            p = probs[g * PER_GROUP + h].astype(BF16)
            outs.append(dot(values_t[h * HEAD_DIM : (h + 1) * HEAD_DIM], p, ((1,), (0,))))
        attn_t = jnp.concatenate(outs, axis=0).astype(BF16)
        return dot(attn_t, gw[...].reshape(cells_here, -1), ((1,), (0,)))

    def back(g):
        keys, queries, values = part(kw, g), part(qw, g), part(vw, g)
        keys_t = keys.T
        d_rows = dw[g]
        dq, dk, dv = [], 0.0, 0.0
        for h in range(PER_GROUP):
            p = probs[g * PER_GROUP + h]
            d_h, q_h = d_rows * pick[h], queries * pick[h]
            dp = dot(values, d_h, ((1,), (1,)))
            delta = jnp.sum(p * dp, axis=0, keepdims=True)
            ds = (p * (dp - delta)).astype(BF16)
            dv = dv + dot(p.astype(BF16), d_h, ((1,), (0,)))
            dk = dk + dot(ds, q_h, ((1,), (0,)))
            dq.append(dot(keys_t[h * HEAD_DIM : (h + 1) * HEAD_DIM], ds, ((1,), (0,))))
        dq = (jnp.concatenate(dq, axis=0) * scale).T
        at_g = slice(g * LANES, (g + 1) * LANES)
        for ref, out, val in ((gq, oq, dq), (gk, ok, dk * scale), (gv, ov, dv)):
            val = val.astype(BF16).reshape(side, row, LANES)
            ref[:, :, at_g] = val
            out[hs:, hr:, at_g] = val[:hs, :hr]

    returning = []

    def give_back():
        for f, (src, dst) in enumerate(((gq, oq), (gk, ok), (gv, ov))):
            for n, (home, here) in enumerate(leaving):
                returning.append(
                    pltpu.make_async_remote_copy(
                        src_ref=src.at[here], dst_ref=dst.at[home],
                        send_sem=out_send.at[f, n], recv_sem=out_recv.at[f, n],
                        device_id=ahead[n], device_id_type=MESH,
                    )
                )
                returning[-1].start()

    arrive(0)
    arrive(1)
    for g in range(groups):
        attend(g)
    arrive(2)
    arrive(3)
    if share:
        (tb, sb, r0, s1, s1b, r1, s2, r2, a2, a1, a0) = scratch[14:25]
        (rep_s, rep_r, tx_s, tx_r, ty_s, ty_r, gy_s, gy_r, gx_s, gx_r, gr_s, gr_r) = scratch[25:]
    rep_copies = []
    half = w_ref.shape[1] // 2
    for g in range(groups):
        term = mix(g)
        at_g = slice(g * LANES, (g + 1) * LANES)
        if not share:
            ow[at_g, :] = term
            continue
        for c in range(2):
            tb[c, at_g] = term[:, c * half : (c + 1) * half]
            sb[c, at_g] = term[:, c * half : (c + 1) * half].astype(BF16)
        rep_copies.append(
            pltpu.make_async_remote_copy(
                src_ref=sb.at[1 - rep, at_g], dst_ref=r0.at[at_g],
                send_sem=rep_s.at[g], recv_sem=rep_r.at[g],
                device_id={"rep": 1 - rep}, device_id_type=MESH,
            )
        )
        rep_copies[-1].start()
    for g in range(groups):
        dw[g] = dot(gw[...].reshape(cells_here, -1), w_ref[g * LANES : (g + 1) * LANES, :], ((1,), (1,))).astype(BF16)

    sent = []

    def spread(src_of, dst_of, peers, send, recv):
        copies = []
        for d, peer in peers:
            copies.append(
                pltpu.make_async_remote_copy(
                    src_ref=src_of(d), dst_ref=dst_of(d),
                    send_sem=send.at[d - 1], recv_sem=recv.at[d - 1],
                    device_id=peer, device_id_type=MESH,
                )
            )
            copies[-1].start()
        sent.extend(copies)
        return copies

    x_peers = [(d, at(d, 0)) for d in range(1, nx)]
    y_peers = [(d, at(0, d)) for d in range(1, ny)]

    back(0)
    if share:
        for copy in rep_copies:
            copy.wait_recv()
        total = tb[rep] + r0[...].astype(F32)
        s1[...] = total.reshape(s1.shape)
        s1b[...] = total.astype(BF16).reshape(s1.shape)
        x_copies = spread(
            lambda d: s1b.at[lax.rem(tx + d, nx)], lambda d: r1.at[d - 1], x_peers, tx_s, tx_r
        )
    back(1)
    if share:
        total = s1[tx]
        for d, copy in enumerate(x_copies):
            copy.wait_recv()
            total = total + r1[d].astype(F32)
        s2[...] = total.reshape(s2.shape)
        y_copies = spread(
            lambda d: s2.at[lax.rem(ty + d, ny)], lambda d: r2.at[d - 1], y_peers, ty_s, ty_r
        )
    back(2)
    for g in range(3, groups):
        back(g)
    give_back()
    if share:
        total = s2[ty]
        for d, copy in enumerate(y_copies):
            copy.wait_recv()
            total = total + r2[d]
        a2[ty] = total * (1.0 / math.sqrt(cells))
        for copy in spread(lambda d: a2.at[ty], lambda d: a2.at[ty], y_peers, gy_s, gy_r):
            copy.wait_recv()
        a1[tx] = a2[...].reshape(a1.shape[1:]).astype(BF16)
        for copy in spread(lambda d: a1.at[tx], lambda d: a1.at[tx], x_peers, gx_s, gx_r):
            copy.wait_recv()
        a0[rep] = a1[...].reshape(a0.shape[1:])
        last = pltpu.make_async_remote_copy(
            src_ref=a0.at[rep], dst_ref=a0.at[rep], send_sem=gr_s, recv_sem=gr_r,
            device_id={"rep": 1 - rep}, device_id_type=MESH,
        )
        last.start()
        last.wait_recv()
        for c in range(2):
            ow[:, c * half : (c + 1) * half] = a0[c].astype(F32)
        sent.append(last)
    for copy in returning:
        copy.wait_recv()
    for copies in arriving:
        sent.extend(copies)
    for copy in sent + returning + rep_copies:
        copy.wait_send()


def local(sizes, queries, keys, values, grad_out, w_out, fluid_count):
    nr, nx, ny = sizes
    side, depth = queries.shape[1], queries.shape[3]
    row, width, model = side * depth, queries.shape[4], grad_out.shape[4]
    cells = side * row * queries.shape[0] * nr * nx * ny
    share = nr == 2 and width % (nx * ny * 8) == 0
    groups = width // LANES
    half = model // 2
    win = pltpu.VMEM((side, row, width), BF16)
    dma = pltpu.SemaphoreType.DMA
    scratch = [
        win, win, win, pltpu.VMEM((side, row, model), BF16),
        pltpu.VMEM((groups * PER_GROUP, side * row, side * row), F32),
        pltpu.VMEM((groups, side * row, LANES), BF16),
        win, win, win,
        dma((4, 3)), dma((4, 3)), dma((4,)), dma((3, 3)), dma((3, 3)),
    ]
    if share:
        wx = width // nx
        wy = wx // ny
        scratch += [
            pltpu.VMEM((2, width, half), F32), pltpu.VMEM((2, width, half), BF16),
            pltpu.VMEM((width, half), BF16),
            pltpu.VMEM((nx, wx, half), F32), pltpu.VMEM((nx, wx, half), BF16),
            pltpu.VMEM((nx - 1, wx, half), BF16),
            pltpu.VMEM((ny, wy, half), F32), pltpu.VMEM((ny - 1, wy, half), F32),
            pltpu.VMEM((ny, wy, half), F32),
            pltpu.VMEM((nx, wx, half), BF16),
            pltpu.VMEM((2, width, half), BF16),
            dma((groups,)), dma((groups,)),
            dma((nx - 1,)), dma((nx - 1,)), dma((ny - 1,)), dma((ny - 1,)),
            dma((ny - 1,)), dma((ny - 1,)), dma((nx - 1,)), dma((nx - 1,)),
            dma, dma,
        ]
    flat = lambda a: a.reshape(side, row, a.shape[-1])
    vmem = pl.BlockSpec(memory_space=pltpu.VMEM)
    hbm = pl.BlockSpec(memory_space=pl.ANY)
    grad = jax.ShapeDtypeStruct((side, row, width), BF16)
    gq, gk, gv, gw = pl.pallas_call(
        functools.partial(kernel, (nx, ny, share, cells)),
        out_shape=(grad, grad, grad, jax.ShapeDtypeStruct((width, model), F32)),
        in_specs=[pl.BlockSpec(memory_space=pltpu.SMEM), hbm, hbm, hbm, hbm, vmem],
        out_specs=(vmem, vmem, vmem, vmem),
        scratch_shapes=scratch,
        compiler_params=pltpu.CompilerParams(
            collective_id=0, has_side_effects=True, vmem_limit_bytes=40 * 2**20
        ),
    )(fluid_count, flat(queries), flat(keys), flat(values), flat(grad_out), w_out)
    if not share:
        gw = lax.psum(gw, ("rep", "tx", "ty")) * (1.0 / math.sqrt(cells))
    back = lambda a: a.reshape(queries.shape)
    return back(gq), back(gk), back(gv), gw


def solution(mesh):
    tile = P("rep", "tx", "ty", None, None)
    sizes = (mesh.shape["rep"], mesh.shape["tx"], mesh.shape["ty"])
    return jax.shard_map(
        functools.partial(local, sizes),
        mesh=mesh,
        in_specs=(tile, tile, tile, tile, P(), P("tx", "ty")),
        out_specs=(tile, tile, tile, P()),
        check_vma=False,
    )
```

```python
import functools
import math

import jax
import jax.numpy as jnp
from jax import lax
from jax.experimental import pallas as pl
from jax.experimental.pallas import tpu as pltpu
from jax.sharding import PartitionSpec as P

HEAD_DIM = 32
LANES = 128
PER_GROUP = LANES // HEAD_DIM
NEG_FILL = -1e30
MESH = pl.DeviceIdType.MESH
F32 = jnp.float32
BF16 = jnp.bfloat16


def dot(a, b, dims):
    return lax.dot_general(a, b, (dims, ((), ())), preferred_element_type=F32)


def kernel(plan, fluid, q_in, k_in, v_in, g_in, w_ref, oq, ok, ov, ow, *scratch):
    nx, ny, share, cells = plan
    (qw, kw, vw, gw, probs, dw, gq, gk, gv, in_send, in_recv, own_sem, out_send, out_recv) = scratch[:14]
    rep, tx, ty = lax.axis_index("rep"), lax.axis_index("tx"), lax.axis_index("ty")

    def at(dx, dy):
        return {"tx": lax.rem(tx + dx, nx), "ty": lax.rem(ty + dy, ny)}

    ahead = [at(1, 0), at(0, 1), at(1, 1)]
    behind = [at(nx - 1, 0), at(0, ny - 1), at(nx - 1, ny - 1)]
    if share:
        greet = [{"rep": 1 - rep}, ahead[2], behind[2]]
        greet += [at(d, 0) for d in range(1, nx)] + [at(0, d) for d in range(1, ny)]
    else:
        greet = ahead + behind
    barrier = pltpu.get_barrier_semaphore()
    for peer in greet:
        pl.semaphore_signal(barrier, inc=1, device_id=peer, device_id_type=MESH)

    side, row, width = qw.shape
    hs, hr = side // 2, row // 2
    lo = (slice(0, hs), slice(0, hr))
    low_x = (slice(0, hs), slice(hr, row))
    low_y = (slice(hs, side), slice(0, hr))
    high = (slice(hs, side), slice(hr, row))
    leaving = [(low_x, low_y), (low_y, low_x), (lo, high)]

    fields = [(q_in, qw), (k_in, kw), (v_in, vw), (g_in, gw)]
    owns = []
    for f, (src, dst) in enumerate(fields):
        owns.append(pltpu.make_async_copy(src.at[high], dst.at[lo], own_sem.at[f]))
        owns[-1].start()
    pl.semaphore_wait(barrier, len(greet))
    arriving = []
    for f, (src, dst) in enumerate(fields):
        copies = []
        for n, (from_, to) in enumerate(leaving):
            copies.append(
                pltpu.make_async_remote_copy(
                    src_ref=src.at[from_], dst_ref=dst.at[to],
                    send_sem=in_send.at[f, n], recv_sem=in_recv.at[f, n],
                    device_id=behind[n], device_id_type=MESH,
                )
            )
            copies[-1].start()
        arriving.append(copies)

    def arrive(f):
        owns[f].wait()
        for copy in arriving[f]:
            copy.wait_recv()

    cells_here = side * row
    groups = width // LANES
    count = fluid[0, 0]
    key_ok = lax.broadcasted_iota(jnp.int32, (cells_here, 1), 0) < count
    query_ok = jnp.where(lax.broadcasted_iota(jnp.int32, (1, cells_here), 1) < count, 1.0, 0.0)
    lane_head = lax.broadcasted_iota(jnp.int32, (1, LANES), 1) // HEAD_DIM
    pick = [jnp.where(lane_head == h, 1.0, 0.0).astype(BF16) for h in range(PER_GROUP)]
    scale = HEAD_DIM ** (-0.5)

    def part(ref, g):
        return ref[:, :, g * LANES : (g + 1) * LANES].reshape(cells_here, LANES)

    def attend(g):
        keys, queries = part(kw, g), part(qw, g)
        for h in range(PER_GROUP):
            s = dot(keys, queries * pick[h], ((1,), (1,)))
            s = jnp.where(key_ok, s, NEG_FILL)
            e = jnp.exp2((s - jnp.max(s, axis=0, keepdims=True)) * (scale * math.log2(math.e)))
            inv = query_ok / jnp.sum(e, axis=0, keepdims=True)
            probs[g * PER_GROUP + h] = e * inv

    def mix(g):
        values_t = part(vw, g).T
        outs = []
        for h in range(PER_GROUP):
            p = probs[g * PER_GROUP + h].astype(BF16)
            outs.append(dot(values_t[h * HEAD_DIM : (h + 1) * HEAD_DIM], p, ((1,), (0,))))
        attn_t = jnp.concatenate(outs, axis=0).astype(BF16)
        return dot(attn_t, gw[...].reshape(cells_here, -1), ((1,), (0,)))

    def back(g):
        keys, queries, values = part(kw, g), part(qw, g), part(vw, g)
        keys_t = keys.T
        d_rows = dw[g]
        dq, dk, dv = [], 0.0, 0.0
        for h in range(PER_GROUP):
            p = probs[g * PER_GROUP + h]
            d_h, q_h = d_rows * pick[h], queries * pick[h]
            dp = dot(values, d_h, ((1,), (1,)))
            delta = jnp.sum(p * dp, axis=0, keepdims=True)
            ds = (p * (dp - delta)).astype(BF16)
            dv = dv + dot(p.astype(BF16), d_h, ((1,), (0,)))
            dk = dk + dot(ds, q_h, ((1,), (0,)))
            dq.append(dot(keys_t[h * HEAD_DIM : (h + 1) * HEAD_DIM], ds, ((1,), (0,))))
        dq = (jnp.concatenate(dq, axis=0) * scale).T
        at_g = slice(g * LANES, (g + 1) * LANES)
        for ref, out, val in ((gq, oq, dq), (gk, ok, dk * scale), (gv, ov, dv)):
            val = val.astype(BF16).reshape(side, row, LANES)
            ref[:, :, at_g] = val
            out[hs:, hr:, at_g] = val[:hs, :hr]

    returning = []

    def give_back(g):
        at_g = slice(g * LANES, (g + 1) * LANES)
        for f, (src, dst) in enumerate(((gq, oq), (gk, ok), (gv, ov))):
            for n, (home, here) in enumerate(leaving):
                returning.append(
                    pltpu.make_async_remote_copy(
                        src_ref=src.at[(*here, at_g)], dst_ref=dst.at[(*home, at_g)],
                        send_sem=out_send.at[g, f, n], recv_sem=out_recv.at[g, f, n],
                        device_id=ahead[n], device_id_type=MESH,
                    )
                )
                returning[-1].start()

    arrive(0)
    arrive(1)
    for g in range(groups):
        attend(g)
    arrive(2)
    arrive(3)
    if share:
        (tb, sb, r0, s1, s1b, r1, s2, s2b, r2, ag) = scratch[14:24]
        (rep_s, rep_r, tx_s, tx_r, ty_s, ty_r, gy_s, gy_r, gx_s, gx_r, gr_s, gr_r) = scratch[24:]
    rep_copies = []
    half = w_ref.shape[1] // 2
    for g in range(groups):
        term = mix(g)
        at_g = slice(g * LANES, (g + 1) * LANES)
        if not share:
            ow[at_g, :] = term
            continue
        for c in range(2):
            tb[c, at_g] = term[:, c * half : (c + 1) * half]
            sb[c, at_g] = term[:, c * half : (c + 1) * half].astype(BF16)
        rep_copies.append(
            pltpu.make_async_remote_copy(
                src_ref=sb.at[1 - rep, at_g], dst_ref=r0.at[at_g],
                send_sem=rep_s.at[g], recv_sem=rep_r.at[g],
                device_id={"rep": 1 - rep}, device_id_type=MESH,
            )
        )
        rep_copies[-1].start()
    for g in range(groups):
        dw[g] = dot(gw[...].reshape(cells_here, -1), w_ref[g * LANES : (g + 1) * LANES, :], ((1,), (1,))).astype(BF16)

    sent = []

    def spread(src_of, dst_of, peers, send, recv):
        copies = []
        for d, peer in peers:
            copies.append(
                pltpu.make_async_remote_copy(
                    src_ref=src_of(d), dst_ref=dst_of(d),
                    send_sem=send.at[d - 1], recv_sem=recv.at[d - 1],
                    device_id=peer, device_id_type=MESH,
                )
            )
            copies[-1].start()
        sent.extend(copies)
        return copies

    x_peers = [(d, at(d, 0)) for d in range(1, nx)]
    y_peers = [(d, at(0, d)) for d in range(1, ny)]

    back(0)
    give_back(0)
    if share:
        for copy in rep_copies:
            copy.wait_recv()
        total = tb[rep] + r0[...].astype(F32)
        s1[...] = total.reshape(s1.shape)
        s1b[...] = total.astype(BF16).reshape(s1.shape)
        x_copies = spread(
            lambda d: s1b.at[lax.rem(tx + d, nx)], lambda d: r1.at[d - 1], x_peers, tx_s, tx_r
        )
    back(1)
    give_back(1)
    if share:
        total = s1[tx]
        for d, copy in enumerate(x_copies):
            copy.wait_recv()
            total = total + r1[d].astype(F32)
        s2[...] = total.reshape(s2.shape)
        s2b[...] = s2[...].astype(BF16)
        y_copies = spread(
            lambda d: s2b.at[lax.rem(ty + d, ny)], lambda d: r2.at[d - 1], y_peers, ty_s, ty_r
        )
    back(2)
    give_back(2)
    for g in range(3, groups):
        back(g)
        give_back(g)
    if share:
        total = s2[ty]
        for d, copy in enumerate(y_copies):
            copy.wait_recv()
            total = total + r2[d].astype(F32)
        ag[rep, tx, ty] = (total * (1.0 / math.sqrt(cells))).astype(BF16)

        def hand(slot, peer, send, recv):
            copy = pltpu.make_async_remote_copy(
                src_ref=ag.at[slot], dst_ref=ag.at[slot], send_sem=send, recv_sem=recv,
                device_id=peer, device_id_type=MESH,
            )
            copy.start()
            sent.append(copy)
            return copy

        def pass_on(dy):
            slot = (rep, tx, lax.rem(ty + dy, ny))
            for d, peer in x_peers:
                along_x[d, dy] = hand(slot, peer, gx_s.at[d - 1, dy], gx_r.at[d - 1, dy])
            to_core.append(hand(slot, {"rep": 1 - rep}, gr_s.at[0, dy], gr_r.at[0, dy]))

        along_x, to_core = {}, []
        along_y = [
            hand((rep, tx, ty), peer, gy_s.at[d - 1], gy_r.at[d - 1]) for d, peer in y_peers
        ]
        pass_on(0)
        order = list(range(ny - 1, 0, -1))
        for d in range(1, ny):
            along_y[d - 1].wait_recv()
            pass_on(ny - d)
        for dy in [0] + order:
            for d in range(1, nx):
                along_x[d, dy].wait_recv()
                slot = (rep, lax.rem(tx + nx - d, nx), lax.rem(ty + dy, ny))
                to_core.append(hand(slot, {"rep": 1 - rep}, gr_s.at[d, dy], gr_r.at[d, dy]))
        for copy in to_core:
            copy.wait_recv()
        wy = ag.shape[3]
        for c in range(2):
            for i in range(nx):
                for j in range(ny):
                    top = (i * ny + j) * wy
                    ow[top : top + wy, c * half : (c + 1) * half] = ag[c, i, j].astype(F32)
    for copy in returning:
        copy.wait_recv()
    for copies in arriving:
        sent.extend(copies)
    for copy in sent + returning + rep_copies:
        copy.wait_send()


def local(sizes, queries, keys, values, grad_out, w_out, fluid_count):
    nr, nx, ny = sizes
    side, depth = queries.shape[1], queries.shape[3]
    row, width, model = side * depth, queries.shape[4], grad_out.shape[4]
    cells = side * row * queries.shape[0] * nr * nx * ny
    share = nr == 2 and width % (nx * ny * 8) == 0
    groups = width // LANES
    half = model // 2
    win = pltpu.VMEM((side, row, width), BF16)
    dma = pltpu.SemaphoreType.DMA
    scratch = [
        win, win, win, pltpu.VMEM((side, row, model), BF16),
        pltpu.VMEM((groups * PER_GROUP, side * row, side * row), F32),
        pltpu.VMEM((groups, side * row, LANES), BF16),
        win, win, win,
        dma((4, 3)), dma((4, 3)), dma((4,)), dma((groups, 3, 3)), dma((groups, 3, 3)),
    ]
    if share:
        wx = width // nx
        wy = wx // ny
        scratch += [
            pltpu.VMEM((2, width, half), F32), pltpu.VMEM((2, width, half), BF16),
            pltpu.VMEM((width, half), BF16),
            pltpu.VMEM((nx, wx, half), F32), pltpu.VMEM((nx, wx, half), BF16),
            pltpu.VMEM((nx - 1, wx, half), BF16),
            pltpu.VMEM((ny, wy, half), F32), pltpu.VMEM((ny, wy, half), BF16),
            pltpu.VMEM((ny - 1, wy, half), BF16),
            pltpu.VMEM((2, nx, ny, wy, half), BF16),
            dma((groups,)), dma((groups,)),
            dma((nx - 1,)), dma((nx - 1,)), dma((ny - 1,)), dma((ny - 1,)),
            dma((ny - 1,)), dma((ny - 1,)), dma((nx - 1, ny)), dma((nx - 1, ny)),
            dma((nx, ny)), dma((nx, ny)),
        ]
    flat = lambda a: a.reshape(side, row, a.shape[-1])
    vmem = pl.BlockSpec(memory_space=pltpu.VMEM)
    hbm = pl.BlockSpec(memory_space=pl.ANY)
    grad = jax.ShapeDtypeStruct((side, row, width), BF16)
    gq, gk, gv, gw = pl.pallas_call(
        functools.partial(kernel, (nx, ny, share, cells)),
        out_shape=(grad, grad, grad, jax.ShapeDtypeStruct((width, model), F32)),
        in_specs=[pl.BlockSpec(memory_space=pltpu.SMEM), hbm, hbm, hbm, hbm, vmem],
        out_specs=(vmem, vmem, vmem, vmem),
        scratch_shapes=scratch,
        compiler_params=pltpu.CompilerParams(
            collective_id=0, has_side_effects=True, vmem_limit_bytes=40 * 2**20
        ),
    )(fluid_count, flat(queries), flat(keys), flat(values), flat(grad_out), w_out)
    if not share:
        gw = lax.psum(gw, ("rep", "tx", "ty")) * (1.0 / math.sqrt(cells))
    back = lambda a: a.reshape(queries.shape)
    return back(gq), back(gk), back(gv), gw


def solution(mesh):
    tile = P("rep", "tx", "ty", None, None)
    sizes = (mesh.shape["rep"], mesh.shape["tx"], mesh.shape["ty"])
    return jax.shard_map(
        functools.partial(local, sizes),
        mesh=mesh,
        in_specs=(tile, tile, tile, tile, P(), P("tx", "ty")),
        out_specs=(tile, tile, tile, P()),
        check_vma=False,
    )
```

```python
import functools
import math

import jax
import jax.numpy as jnp
from jax import lax
from jax.experimental import pallas as pl
from jax.experimental.pallas import tpu as pltpu
from jax.sharding import PartitionSpec as P

HEAD_DIM = 32
LANES = 128
PER_GROUP = LANES // HEAD_DIM
NEG_FILL = -1e30
MESH = pl.DeviceIdType.MESH
F32 = jnp.float32
BF16 = jnp.bfloat16


def dot(a, b, dims):
    return lax.dot_general(a, b, (dims, ((), ())), preferred_element_type=F32)


def kernel(plan, fluid, qkv, w_ref, oq, ok, ov, ow, *scratch):
    nx, ny, share, cells = plan
    (qw, kw, vw, gw, probs, dw, gq, gk, gv, in_send, in_recv, own_sem, out_send, out_recv) = scratch[:14]
    rep, tx, ty = lax.axis_index("rep"), lax.axis_index("tx"), lax.axis_index("ty")

    def at(dx, dy):
        return {"tx": lax.rem(tx + dx, nx), "ty": lax.rem(ty + dy, ny)}

    ahead = [at(1, 0), at(0, 1), at(1, 1)]
    behind = [at(nx - 1, 0), at(0, ny - 1), at(nx - 1, ny - 1)]
    if share:
        greet = [{"rep": 1 - rep}, ahead[2], behind[2]]
        greet += [at(d, 0) for d in range(1, nx)] + [at(0, d) for d in range(1, ny)]
    else:
        greet = ahead + behind
    barrier = pltpu.get_barrier_semaphore()
    for peer in greet:
        pl.semaphore_signal(barrier, inc=1, device_id=peer, device_id_type=MESH)

    side, row, width = qw.shape
    hs, hr = side // 2, row // 2
    lo = (slice(0, hs), slice(0, hr))
    low_x = (slice(0, hs), slice(hr, row))
    low_y = (slice(hs, side), slice(0, hr))
    high = (slice(hs, side), slice(hr, row))
    leaving = [(low_x, low_y), (low_y, low_x), (lo, high)]

    def third(n):
        return qkv.at[:, :, n * width : (n + 1) * width]

    fields = [(third(0), qw), (third(1), kw), (third(2), vw), (qkv.at[:, :, 3 * width :], gw)]
    owns = []
    for f, (src, dst) in enumerate(fields):
        owns.append(pltpu.make_async_copy(src.at[high], dst.at[lo], own_sem.at[f]))
        owns[-1].start()
    pl.semaphore_wait(barrier, len(greet))
    arriving = []
    for f, (src, dst) in enumerate(fields):
        copies = []
        for n, (from_, to) in enumerate(leaving):
            copies.append(
                pltpu.make_async_remote_copy(
                    src_ref=src.at[from_], dst_ref=dst.at[to],
                    send_sem=in_send.at[f, n], recv_sem=in_recv.at[f, n],
                    device_id=behind[n], device_id_type=MESH,
                )
            )
            copies[-1].start()
        arriving.append(copies)

    def arrive(f):
        owns[f].wait()
        for copy in arriving[f]:
            copy.wait_recv()

    cells_here = side * row
    groups = width // LANES
    count = fluid[0, 0]
    key_ok = lax.broadcasted_iota(jnp.int32, (cells_here, 1), 0) < count
    query_ok = jnp.where(lax.broadcasted_iota(jnp.int32, (1, cells_here), 1) < count, 1.0, 0.0)
    lane_head = lax.broadcasted_iota(jnp.int32, (1, LANES), 1) // HEAD_DIM
    pick = [jnp.where(lane_head == h, 1.0, 0.0).astype(BF16) for h in range(PER_GROUP)]
    scale = HEAD_DIM ** (-0.5)

    def part(ref, g):
        return ref[:, :, g * LANES : (g + 1) * LANES].reshape(cells_here, LANES)

    def attend(g):
        keys, queries = part(kw, g), part(qw, g)
        for h in range(PER_GROUP):
            s = dot(keys, queries * pick[h], ((1,), (1,)))
            s = jnp.where(key_ok, s, NEG_FILL)
            e = jnp.exp2((s - jnp.max(s, axis=0, keepdims=True)) * (scale * math.log2(math.e)))
            inv = query_ok / jnp.sum(e, axis=0, keepdims=True)
            probs[g * PER_GROUP + h] = e * inv

    def mix(g):
        values_t = part(vw, g).T
        outs = []
        for h in range(PER_GROUP):
            p = probs[g * PER_GROUP + h].astype(BF16)
            outs.append(dot(values_t[h * HEAD_DIM : (h + 1) * HEAD_DIM], p, ((1,), (0,))))
        attn_t = jnp.concatenate(outs, axis=0).astype(BF16)
        return dot(attn_t, gw[...].reshape(cells_here, -1), ((1,), (0,)))

    def back(g):
        keys, queries, values = part(kw, g), part(qw, g), part(vw, g)
        keys_t = keys.T
        d_rows = dw[g]
        dq, dk, dv = [], 0.0, 0.0
        for h in range(PER_GROUP):
            p = probs[g * PER_GROUP + h]
            d_h, q_h = d_rows * pick[h], queries * pick[h]
            dp = dot(values, d_h, ((1,), (1,)))
            delta = jnp.sum(p * dp, axis=0, keepdims=True)
            ds = (p * (dp - delta)).astype(BF16)
            dv = dv + dot(p.astype(BF16), d_h, ((1,), (0,)))
            dk = dk + dot(ds, q_h, ((1,), (0,)))
            dq.append(dot(keys_t[h * HEAD_DIM : (h + 1) * HEAD_DIM], ds, ((1,), (0,))))
        dq = (jnp.concatenate(dq, axis=0) * scale).T
        at_g = slice(g * LANES, (g + 1) * LANES)
        for ref, out, val in ((gq, oq, dq), (gk, ok, dk * scale), (gv, ov, dv)):
            val = val.astype(BF16).reshape(side, row, LANES)
            ref[:, :, at_g] = val
            out[hs:, hr:, at_g] = val[:hs, :hr]

    returning = []

    def give_back(g):
        at_g = slice(g * LANES, (g + 1) * LANES)
        for f, (src, dst) in enumerate(((gq, oq), (gk, ok), (gv, ov))):
            for n, (home, here) in enumerate(leaving):
                returning.append(
                    pltpu.make_async_remote_copy(
                        src_ref=src.at[(*here, at_g)], dst_ref=dst.at[(*home, at_g)],
                        send_sem=out_send.at[g, f, n], recv_sem=out_recv.at[g, f, n],
                        device_id=ahead[n], device_id_type=MESH,
                    )
                )
                returning[-1].start()

    arrive(0)
    arrive(1)
    for g in range(groups):
        attend(g)
    arrive(2)
    arrive(3)
    if share:
        (tb, sb, r0, s1, s1b, r1, s2, s2b, r2, ag) = scratch[14:24]
        (rep_s, rep_r, tx_s, tx_r, ty_s, ty_r, gy_s, gy_r, gx_s, gx_r, gr_s, gr_r) = scratch[24:]
    rep_copies = []
    half = w_ref.shape[1] // 2
    for g in range(groups):
        term = mix(g)
        at_g = slice(g * LANES, (g + 1) * LANES)
        if not share:
            ow[at_g, :] = term
            continue
        for c in range(2):
            tb[c, at_g] = term[:, c * half : (c + 1) * half]
            sb[c, at_g] = term[:, c * half : (c + 1) * half].astype(BF16)
        rep_copies.append(
            pltpu.make_async_remote_copy(
                src_ref=sb.at[1 - rep, at_g], dst_ref=r0.at[at_g],
                send_sem=rep_s.at[g], recv_sem=rep_r.at[g],
                device_id={"rep": 1 - rep}, device_id_type=MESH,
            )
        )
        rep_copies[-1].start()
    for g in range(groups):
        dw[g] = dot(gw[...].reshape(cells_here, -1), w_ref[g * LANES : (g + 1) * LANES, :], ((1,), (1,))).astype(BF16)

    sent = []

    def spread(src_of, dst_of, peers, send, recv):
        copies = []
        for d, peer in peers:
            copies.append(
                pltpu.make_async_remote_copy(
                    src_ref=src_of(d), dst_ref=dst_of(d),
                    send_sem=send.at[d - 1], recv_sem=recv.at[d - 1],
                    device_id=peer, device_id_type=MESH,
                )
            )
            copies[-1].start()
        sent.extend(copies)
        return copies

    x_peers = [(d, at(d, 0)) for d in range(1, nx)]
    y_peers = [(d, at(0, d)) for d in range(1, ny)]

    back(0)
    give_back(0)
    if share:
        for copy in rep_copies:
            copy.wait_recv()
        total = tb[rep] + r0[...].astype(F32)
        s1[...] = total.reshape(s1.shape)
        s1b[...] = total.astype(BF16).reshape(s1.shape)
        x_copies = spread(
            lambda d: s1b.at[lax.rem(tx + d, nx)], lambda d: r1.at[d - 1], x_peers, tx_s, tx_r
        )
    back(1)
    give_back(1)
    if share:
        total = s1[tx]
        for d, copy in enumerate(x_copies):
            copy.wait_recv()
            total = total + r1[d].astype(F32)
        s2[...] = total.reshape(s2.shape)
        s2b[...] = s2[...].astype(BF16)
        y_copies = spread(
            lambda d: s2b.at[lax.rem(ty + d, ny)], lambda d: r2.at[d - 1], y_peers, ty_s, ty_r
        )
    back(2)
    give_back(2)
    for g in range(3, groups):
        back(g)
        give_back(g)
    if share:
        total = s2[ty]
        for d, copy in enumerate(y_copies):
            copy.wait_recv()
            total = total + r2[d].astype(F32)
        ag[rep, tx, ty] = (total * (1.0 / math.sqrt(cells))).astype(BF16)

        def hand(slot, peer, send, recv):
            copy = pltpu.make_async_remote_copy(
                src_ref=ag.at[slot], dst_ref=ag.at[slot], send_sem=send, recv_sem=recv,
                device_id=peer, device_id_type=MESH,
            )
            copy.start()
            sent.append(copy)
            return copy

        def pass_on(dy):
            slot = (rep, tx, lax.rem(ty + dy, ny))
            for d, peer in x_peers:
                along_x[d, dy] = hand(slot, peer, gx_s.at[d - 1, dy], gx_r.at[d - 1, dy])
            to_core.append(hand(slot, {"rep": 1 - rep}, gr_s.at[0, dy], gr_r.at[0, dy]))

        along_x, to_core = {}, []
        along_y = [
            hand((rep, tx, ty), peer, gy_s.at[d - 1], gy_r.at[d - 1]) for d, peer in y_peers
        ]
        pass_on(0)
        order = list(range(ny - 1, 0, -1))
        for d in range(1, ny):
            along_y[d - 1].wait_recv()
            pass_on(ny - d)
        for dy in [0] + order:
            for d in range(1, nx):
                along_x[d, dy].wait_recv()
                slot = (rep, lax.rem(tx + nx - d, nx), lax.rem(ty + dy, ny))
                to_core.append(hand(slot, {"rep": 1 - rep}, gr_s.at[d, dy], gr_r.at[d, dy]))
        for copy in to_core:
            copy.wait_recv()
        wy = ag.shape[3]
        for c in range(2):
            for i in range(nx):
                for j in range(ny):
                    top = (i * ny + j) * wy
                    ow[top : top + wy, c * half : (c + 1) * half] = ag[c, i, j].astype(F32)
    for copy in returning:
        copy.wait_recv()
    for copies in arriving:
        sent.extend(copies)
    for copy in sent + returning + rep_copies:
        copy.wait_send()


def local(sizes, queries, keys, values, grad_out, w_out, fluid_count):
    nr, nx, ny = sizes
    side, depth = queries.shape[1], queries.shape[3]
    row, width, model = side * depth, queries.shape[4], grad_out.shape[4]
    cells = side * row * queries.shape[0] * nr * nx * ny
    share = nr == 2 and width % (nx * ny * 8) == 0
    groups = width // LANES
    half = model // 2
    win = pltpu.VMEM((side, row, width), BF16)
    dma = pltpu.SemaphoreType.DMA
    scratch = [
        win, win, win, pltpu.VMEM((side, row, model), BF16),
        pltpu.VMEM((groups * PER_GROUP, side * row, side * row), F32),
        pltpu.VMEM((groups, side * row, LANES), BF16),
        win, win, win,
        dma((4, 3)), dma((4, 3)), dma((4,)), dma((groups, 3, 3)), dma((groups, 3, 3)),
    ]
    if share:
        wx = width // nx
        wy = wx // ny
        scratch += [
            pltpu.VMEM((2, width, half), F32), pltpu.VMEM((2, width, half), BF16),
            pltpu.VMEM((width, half), BF16),
            pltpu.VMEM((nx, wx, half), F32), pltpu.VMEM((nx, wx, half), BF16),
            pltpu.VMEM((nx - 1, wx, half), BF16),
            pltpu.VMEM((ny, wy, half), F32), pltpu.VMEM((ny, wy, half), BF16),
            pltpu.VMEM((ny - 1, wy, half), BF16),
            pltpu.VMEM((2, nx, ny, wy, half), BF16),
            dma((groups,)), dma((groups,)),
            dma((nx - 1,)), dma((nx - 1,)), dma((ny - 1,)), dma((ny - 1,)),
            dma((ny - 1,)), dma((ny - 1,)), dma((nx - 1, ny)), dma((nx - 1, ny)),
            dma((nx, ny)), dma((nx, ny)),
        ]
    flat = lambda a: a.reshape(side, row, a.shape[-1])
    vmem = pl.BlockSpec(memory_space=pltpu.VMEM)
    hbm = pl.BlockSpec(memory_space=pl.ANY)
    grad = jax.ShapeDtypeStruct((side, row, width), BF16)
    gq, gk, gv, gw = pl.pallas_call(
        functools.partial(kernel, (nx, ny, share, cells)),
        out_shape=(grad, grad, grad, jax.ShapeDtypeStruct((width, model), F32)),
        in_specs=[pl.BlockSpec(memory_space=pltpu.SMEM), hbm, vmem],
        out_specs=(vmem, vmem, vmem, vmem),
        scratch_shapes=scratch,
        compiler_params=pltpu.CompilerParams(
            collective_id=0, has_side_effects=True, vmem_limit_bytes=40 * 2**20
        ),
    )(fluid_count, flat(jnp.concatenate([queries, keys, values, grad_out], axis=4)), w_out)
    if not share:
        gw = lax.psum(gw, ("rep", "tx", "ty")) * (1.0 / math.sqrt(cells))
    back = lambda a: a.reshape(queries.shape)
    return back(gq), back(gk), back(gv), gw


def solution(mesh):
    tile = P("rep", "tx", "ty", None, None)
    sizes = (mesh.shape["rep"], mesh.shape["tx"], mesh.shape["ty"])
    return jax.shard_map(
        functools.partial(local, sizes),
        mesh=mesh,
        in_specs=(tile, tile, tile, tile, P(), P("tx", "ty")),
        out_specs=(tile, tile, tile, P()),
        check_vma=False,
    )
```

```python
import functools
import math

import jax
import jax.numpy as jnp
from jax import lax
from jax.experimental import pallas as pl
from jax.experimental.pallas import tpu as pltpu
from jax.sharding import PartitionSpec as P

HEAD_DIM = 32
LANES = 128
PER_GROUP = LANES // HEAD_DIM
NEG_FILL = -1e30
MESH = pl.DeviceIdType.MESH
F32 = jnp.float32
BF16 = jnp.bfloat16


def dot(a, b, dims):
    return lax.dot_general(a, b, (dims, ((), ())), preferred_element_type=F32)


def kernel(plan, fluid, qkv, w_ref, oq, ok, ov, ow, *scratch):
    nx, ny, share, cells = plan
    (qw, kw, vw, gw, probs, dw, gq, gk, gv, in_send, in_recv, own_sem, out_send, out_recv) = scratch[:14]
    rep, tx, ty = lax.axis_index("rep"), lax.axis_index("tx"), lax.axis_index("ty")

    def at(dx, dy):
        return {"tx": lax.rem(tx + dx, nx), "ty": lax.rem(ty + dy, ny)}

    ahead = [at(1, 0), at(0, 1), at(1, 1)]
    behind = [at(nx - 1, 0), at(0, ny - 1), at(nx - 1, ny - 1)]
    if share:
        greet = [{"rep": 1 - rep}, ahead[2], behind[2]]
        greet += [at(d, 0) for d in range(1, nx)] + [at(0, d) for d in range(1, ny)]
    else:
        greet = ahead + behind
    barrier = pltpu.get_barrier_semaphore()
    for peer in greet:
        pl.semaphore_signal(barrier, inc=1, device_id=peer, device_id_type=MESH)

    side, row, width = qw.shape
    hs, hr = side // 2, row // 2
    lo = (slice(0, hs), slice(0, hr))
    low_x = (slice(0, hs), slice(hr, row))
    low_y = (slice(hs, side), slice(0, hr))
    high = (slice(hs, side), slice(hr, row))
    leaving = [(low_x, low_y), (low_y, low_x), (lo, high)]

    def third(n):
        return qkv.at[:, :, n * width : (n + 1) * width]

    fields = [(third(0), qw), (third(1), kw), (third(2), vw), (qkv.at[:, :, 3 * width :], gw)]
    owns = []
    for f, (src, dst) in enumerate(fields):
        owns.append(pltpu.make_async_copy(src.at[high], dst.at[lo], own_sem.at[f]))
        owns[-1].start()
    pl.semaphore_wait(barrier, len(greet))
    arriving = []
    for f, (src, dst) in enumerate(fields):
        copies = []
        for n, (from_, to) in enumerate(leaving):
            copies.append(
                pltpu.make_async_remote_copy(
                    src_ref=src.at[from_], dst_ref=dst.at[to],
                    send_sem=in_send.at[f, n], recv_sem=in_recv.at[f, n],
                    device_id=behind[n], device_id_type=MESH,
                )
            )
            copies[-1].start()
        arriving.append(copies)

    def arrive(f):
        owns[f].wait()
        for copy in arriving[f]:
            copy.wait_recv()

    cells_here = side * row
    groups = width // LANES
    count = fluid[0, 0]
    key_ok = lax.broadcasted_iota(jnp.int32, (cells_here, 1), 0) < count
    query_ok = jnp.where(lax.broadcasted_iota(jnp.int32, (1, cells_here), 1) < count, 1.0, 0.0)
    lane_head = lax.broadcasted_iota(jnp.int32, (1, LANES), 1) // HEAD_DIM
    pick = [jnp.where(lane_head == h, 1.0, 0.0).astype(BF16) for h in range(PER_GROUP)]
    scale = HEAD_DIM ** (-0.5)

    def part(ref, g):
        return ref[:, :, g * LANES : (g + 1) * LANES].reshape(cells_here, LANES)

    def attend(g):
        keys, queries = part(kw, g), part(qw, g)
        for h in range(PER_GROUP):
            s = dot(keys, queries * pick[h], ((1,), (1,)))
            s = jnp.where(key_ok, s, NEG_FILL)
            e = jnp.exp2((s - jnp.max(s, axis=0, keepdims=True)) * (scale * math.log2(math.e)))
            inv = query_ok / jnp.sum(e, axis=0, keepdims=True)
            probs[g * PER_GROUP + h] = e * inv

    def mix(g):
        values_t = part(vw, g).T
        outs = []
        for h in range(PER_GROUP):
            p = probs[g * PER_GROUP + h].astype(BF16)
            outs.append(dot(values_t[h * HEAD_DIM : (h + 1) * HEAD_DIM], p, ((1,), (0,))))
        attn_t = jnp.concatenate(outs, axis=0).astype(BF16)
        return dot(attn_t, gw[...].reshape(cells_here, -1), ((1,), (0,)))

    def back(g):
        keys, queries, values = part(kw, g), part(qw, g), part(vw, g)
        keys_t = keys.T
        d_rows = dw[g]
        dq, dk, dv = [], 0.0, 0.0
        for h in range(PER_GROUP):
            p = probs[g * PER_GROUP + h]
            d_h, q_h = d_rows * pick[h], queries * pick[h]
            dp = dot(values, d_h, ((1,), (1,)))
            delta = jnp.sum(p * dp, axis=0, keepdims=True)
            ds = (p * (dp - delta)).astype(BF16)
            dv = dv + dot(p.astype(BF16), d_h, ((1,), (0,)))
            dk = dk + dot(ds, q_h, ((1,), (0,)))
            dq.append(dot(keys_t[h * HEAD_DIM : (h + 1) * HEAD_DIM], ds, ((1,), (0,))))
        dq = (jnp.concatenate(dq, axis=0) * scale).T
        at_g = slice(g * LANES, (g + 1) * LANES)
        for ref, out, val in ((gq, oq, dq), (gk, ok, dk * scale), (gv, ov, dv)):
            val = val.astype(BF16).reshape(side, row, LANES)
            ref[:, :, at_g] = val
            out[hs:, hr:, at_g] = val[:hs, :hr]

    returning = []

    def give_back(g):
        at_g = slice(g * LANES, (g + 1) * LANES)
        for f, (src, dst) in enumerate(((gq, oq), (gk, ok), (gv, ov))):
            for n, (home, here) in enumerate(leaving):
                returning.append(
                    pltpu.make_async_remote_copy(
                        src_ref=src.at[(*here, at_g)], dst_ref=dst.at[(*home, at_g)],
                        send_sem=out_send.at[g, f, n], recv_sem=out_recv.at[g, f, n],
                        device_id=ahead[n], device_id_type=MESH,
                    )
                )
                returning[-1].start()

    arrive(0)
    arrive(1)
    for g in range(groups):
        attend(g)
    arrive(2)
    arrive(3)
    if share:
        (tb, sb, r0, s1, s1b, r1, s2, s2b, r2, ag) = scratch[14:24]
        (rep_s, rep_r, tx_s, tx_r, ty_s, ty_r, gy_s, gy_r, gx_s, gx_r, gr_s, gr_r) = scratch[24:]
    rep_copies = []
    half = w_ref.shape[1] // 2
    for g in range(groups):
        term = mix(g)
        at_g = slice(g * LANES, (g + 1) * LANES)
        if not share:
            ow[at_g, :] = term
            continue
        for c in range(2):
            tb[c, at_g] = term[:, c * half : (c + 1) * half]
            sb[c, at_g] = term[:, c * half : (c + 1) * half].astype(BF16)
        rep_copies.append(
            pltpu.make_async_remote_copy(
                src_ref=sb.at[1 - rep, at_g], dst_ref=r0.at[at_g],
                send_sem=rep_s.at[g], recv_sem=rep_r.at[g],
                device_id={"rep": 1 - rep}, device_id_type=MESH,
            )
        )
        rep_copies[-1].start()
    for g in range(groups):
        dw[g] = dot(gw[...].reshape(cells_here, -1), w_ref[g * LANES : (g + 1) * LANES, :], ((1,), (1,))).astype(BF16)

    sent = []

    def spread(src_of, dst_of, peers, send, recv):
        copies = []
        for d, peer in peers:
            copies.append(
                pltpu.make_async_remote_copy(
                    src_ref=src_of(d), dst_ref=dst_of(d),
                    send_sem=send.at[d - 1], recv_sem=recv.at[d - 1],
                    device_id=peer, device_id_type=MESH,
                )
            )
            copies[-1].start()
        sent.extend(copies)
        return copies

    x_peers = [(d, at(d, 0)) for d in range(1, nx)]
    y_peers = [(d, at(0, d)) for d in range(1, ny)]

    back(0)
    if share:
        for copy in rep_copies:
            copy.wait_recv()
        total = tb[rep] + r0[...].astype(F32)
        s1[...] = total.reshape(s1.shape)
        s1b[...] = total.astype(BF16).reshape(s1.shape)
        x_copies = spread(
            lambda d: s1b.at[lax.rem(tx + d, nx)], lambda d: r1.at[d - 1], x_peers, tx_s, tx_r
        )
    give_back(0)
    back(1)
    if share:
        total = s1[tx]
        for d, copy in enumerate(x_copies):
            copy.wait_recv()
            total = total + r1[d].astype(F32)
        s2[...] = total.reshape(s2.shape)
        s2b[...] = s2[...].astype(BF16)
        y_copies = spread(
            lambda d: s2b.at[lax.rem(ty + d, ny)], lambda d: r2.at[d - 1], y_peers, ty_s, ty_r
        )
    give_back(1)
    back(2)
    if not share:
        give_back(2)
    for g in range(3, groups):
        back(g)
        give_back(g)
    if share:
        total = s2[ty]
        for d, copy in enumerate(y_copies):
            copy.wait_recv()
            total = total + r2[d].astype(F32)
        ag[rep, tx, ty] = (total * (1.0 / math.sqrt(cells))).astype(BF16)

        def hand(slot, peer, send, recv):
            copy = pltpu.make_async_remote_copy(
                src_ref=ag.at[slot], dst_ref=ag.at[slot], send_sem=send, recv_sem=recv,
                device_id=peer, device_id_type=MESH,
            )
            copy.start()
            sent.append(copy)
            return copy

        def pass_on(dy):
            slot = (rep, tx, lax.rem(ty + dy, ny))
            for d, peer in x_peers:
                along_x[d, dy] = hand(slot, peer, gx_s.at[d - 1, dy], gx_r.at[d - 1, dy])
            to_core.append(hand(slot, {"rep": 1 - rep}, gr_s.at[0, dy], gr_r.at[0, dy]))

        along_x, to_core = {}, []
        along_y = [
            hand((rep, tx, ty), peer, gy_s.at[d - 1], gy_r.at[d - 1]) for d, peer in y_peers
        ]
        pass_on(0)
        give_back(2)
        order = list(range(ny - 1, 0, -1))
        for d in range(1, ny):
            along_y[d - 1].wait_recv()
            pass_on(ny - d)
        for dy in [0] + order:
            for d in range(1, nx):
                along_x[d, dy].wait_recv()
                slot = (rep, lax.rem(tx + nx - d, nx), lax.rem(ty + dy, ny))
                to_core.append(hand(slot, {"rep": 1 - rep}, gr_s.at[d, dy], gr_r.at[d, dy]))
        for copy in to_core:
            copy.wait_recv()
        wy = ag.shape[3]
        for c in range(2):
            for i in range(nx):
                for j in range(ny):
                    top = (i * ny + j) * wy
                    ow[top : top + wy, c * half : (c + 1) * half] = ag[c, i, j].astype(F32)
    for copy in returning:
        copy.wait_recv()
    for copies in arriving:
        sent.extend(copies)
    for copy in sent + returning + rep_copies:
        copy.wait_send()


def local(sizes, queries, keys, values, grad_out, w_out, fluid_count):
    nr, nx, ny = sizes
    side, depth = queries.shape[1], queries.shape[3]
    row, width, model = side * depth, queries.shape[4], grad_out.shape[4]
    cells = side * row * queries.shape[0] * nr * nx * ny
    share = nr == 2 and width % (nx * ny * 8) == 0
    groups = width // LANES
    half = model // 2
    win = pltpu.VMEM((side, row, width), BF16)
    dma = pltpu.SemaphoreType.DMA
    scratch = [
        win, win, win, pltpu.VMEM((side, row, model), BF16),
        pltpu.VMEM((groups * PER_GROUP, side * row, side * row), F32),
        pltpu.VMEM((groups, side * row, LANES), BF16),
        win, win, win,
        dma((4, 3)), dma((4, 3)), dma((4,)), dma((groups, 3, 3)), dma((groups, 3, 3)),
    ]
    if share:
        wx = width // nx
        wy = wx // ny
        scratch += [
            pltpu.VMEM((2, width, half), F32), pltpu.VMEM((2, width, half), BF16),
            pltpu.VMEM((width, half), BF16),
            pltpu.VMEM((nx, wx, half), F32), pltpu.VMEM((nx, wx, half), BF16),
            pltpu.VMEM((nx - 1, wx, half), BF16),
            pltpu.VMEM((ny, wy, half), F32), pltpu.VMEM((ny, wy, half), BF16),
            pltpu.VMEM((ny - 1, wy, half), BF16),
            pltpu.VMEM((2, nx, ny, wy, half), BF16),
            dma((groups,)), dma((groups,)),
            dma((nx - 1,)), dma((nx - 1,)), dma((ny - 1,)), dma((ny - 1,)),
            dma((ny - 1,)), dma((ny - 1,)), dma((nx - 1, ny)), dma((nx - 1, ny)),
            dma((nx, ny)), dma((nx, ny)),
        ]
    flat = lambda a: a.reshape(side, row, a.shape[-1])
    vmem = pl.BlockSpec(memory_space=pltpu.VMEM)
    hbm = pl.BlockSpec(memory_space=pl.ANY)
    grad = jax.ShapeDtypeStruct((side, row, width), BF16)
    gq, gk, gv, gw = pl.pallas_call(
        functools.partial(kernel, (nx, ny, share, cells)),
        out_shape=(grad, grad, grad, jax.ShapeDtypeStruct((width, model), F32)),
        in_specs=[pl.BlockSpec(memory_space=pltpu.SMEM), hbm, vmem],
        out_specs=(vmem, vmem, vmem, vmem),
        scratch_shapes=scratch,
        compiler_params=pltpu.CompilerParams(
            collective_id=0, has_side_effects=True, vmem_limit_bytes=40 * 2**20
        ),
    )(fluid_count, flat(jnp.concatenate([queries, keys, values, grad_out], axis=4)), w_out)
    if not share:
        gw = lax.psum(gw, ("rep", "tx", "ty")) * (1.0 / math.sqrt(cells))
    back = lambda a: a.reshape(queries.shape)
    return back(gq), back(gk), back(gv), gw


def solution(mesh):
    tile = P("rep", "tx", "ty", None, None)
    sizes = (mesh.shape["rep"], mesh.shape["tx"], mesh.shape["ty"])
    return jax.shard_map(
        functools.partial(local, sizes),
        mesh=mesh,
        in_specs=(tile, tile, tile, tile, P(), P("tx", "ty")),
        out_specs=(tile, tile, tile, P()),
        check_vma=False,
    )
```
